32 devices in a mesh: groups: 2 (over y), row: 2 (over core), col: 8 (over z, x).
Axes of the slice: x: 2, y: 2, z: 4, core: 2. Of those that a mesh axis runs over, the one named last changes fastest.
Arguments:
- inputs: bfloat16 [512, 2, 6144], P(('groups', 'row'), None, 'col'), parts along dimension 0, may hold values from -6 to 6
- weights: bfloat16 [12288, 24576], P('row', 'col'), may hold values from -0.0546875 to 0.0546875
- grad_act: bfloat16 [512, 24576], P(('groups', 'row'), 'col'), parts along dimension 0, may hold values from -6 to 6
Outputs:
- activation: bfloat16 [512, 24576], P(('groups', 'row'), 'col'), parts along dimension 0
- grad_x: bfloat16 [512, 2, 6144], P(('groups', 'row'), None, 'col'), parts along dimension 0
- grad_w: bfloat16 [24576, 24576], P(('groups', 'row'), 'col'), parts along dimension 0
The draws below stay inside these ranges and needn't reach their ends.
There are 2 independent parts, one for each index of `groups`. The reference program is written for one: setup_inputs(seed, part) draws one part's arguments, and reference() takes and returns one part's arrays. A program takes and returns all parts, laid end to end along the dimension named above; an argument that names none is the same for every part. Nothing has to cross between parts.
All inputs are finite; a program needn't handle non-finite values.
Results may differ from the reference program's by a relative error of at most 0.0049.
Values may be sent and summed in bfloat16 or wider, within the bound.
A program may use at most 448 MiB of HBM per device.

```python
import math
import jax
import jax.numpy as jnp

D = 12288
FFW = 24576
TOKENS = 256
N_ROW = 2


def shard_levels(rng, extent, pieces, least, largest):
    gain, own = 1.0, jax.random.fold_in(rng, 6)
    for position, parts in pieces:
        heights = jnp.exp(jax.random.uniform(jax.random.fold_in(own, position), (parts,), jnp.float32, least / len(pieces), largest / len(pieces)))
        gain = gain * jnp.repeat(heights, extent[position] // parts).reshape([-1 if axis == position else 1 for axis in range(len(extent))])
    return gain


def scatter_about(rng, dims, spread, reach, cuts=(), held_as=jnp.bfloat16):
    array = jax.random.normal(rng, dims, jnp.float32) * spread
    if len(cuts) > 0:
        array = shard_levels(rng, dims, cuts, -0.22, 0.18) * array
    return jnp.clip(array, min=-reach, max=reach).astype(held_as)


def setup_inputs(seed: int = 0, part: int = 0) -> dict:
    seeds = jax.random.split(jax.random.key(seed), 4)
    own_keys = jax.random.split(jax.random.fold_in(seeds[3], part), 4)
    return {
        "inputs": scatter_about(own_keys[0], (TOKENS, N_ROW, D // N_ROW), 1.0, 6.0, ((0, 2), (2, 8))),
        "weights": scatter_about(seeds[1], (D, FFW), D ** -0.5, 0.0546875, ((0, 2), (1, 8))),
        "grad_act": scatter_about(own_keys[2], (TOKENS, FFW), 1.0, 6.0, ((0, 2), (1, 8))),
    }


root_coef = math.sqrt(2.0 / math.pi)
cube_coef = 0.044715

def tanh_gelu(preact):
    tanh_arg = root_coef * (preact + cube_coef * preact * preact * preact)
    return 0.5 * preact * (1.0 + jnp.tanh(tanh_arg))

def gelu_slope(preact):
    tanh_arg = root_coef * (preact + cube_coef * preact * preact * preact)
    tangent = jnp.tanh(tanh_arg)
    return 0.5 * (1.0 + tangent) + 0.5 * preact * (1.0 - tangent * tangent) * root_coef * (1.0 + 3.0 * cube_coef * preact * preact)

def reference(inputs, weights, grad_act):
    flat_inputs = inputs.reshape(TOKENS, D)
    preact = jnp.dot(flat_inputs, weights, preferred_element_type=jnp.float32)
    activation = tanh_gelu(preact).astype(jnp.bfloat16)
    grad_pre = (grad_act.astype(jnp.float32) * gelu_slope(preact)).astype(jnp.bfloat16)
    grad_w = jnp.dot(flat_inputs.T, grad_pre, preferred_element_type=jnp.float32).astype(jnp.bfloat16)
    grad_x = jnp.dot(grad_pre, weights.T, preferred_element_type=jnp.float32).astype(jnp.bfloat16)
    return (activation, grad_x.reshape(TOKENS, N_ROW, D // N_ROW), grad_w)
```

```python
import functools
import math

import jax
import jax.numpy as jnp
from jax import lax
from jax.experimental import pallas as pl
from jax.experimental.pallas import tpu as pltpu
from jax.sharding import PartitionSpec as P

root_coef = math.sqrt(2.0 / math.pi)
cube_coef = 0.044715
MESH = pl.DeviceIdType.MESH


def gelu_parts(preact):
    square = preact * preact
    tangent = jnp.tanh(root_coef * (preact + cube_coef * square * preact))
    half = 0.5 * (1.0 + tangent)
    slope = half + 0.5 * preact * (1.0 - tangent * tangent) * root_coef * (
        1.0 + 3.0 * cube_coef * square
    )
    return preact * half, slope


def ring_place(index, count):
    z, x = index // 2, index % 2
    return z * (1 - x) + (count - 1 - z) * x


def ring_column(place, count):
    place = lax.rem(place + 2 * count, count)
    back = place // (count // 2)
    return (1 - back) * (2 * place) + back * (2 * (count - 1 - place) + 1)


def exchange_kernel(
    count, tile, split,
    x_ref, w_ref, ga_ref,
    act_ref, own_ref, gradall_ref, sum_ref, term_ref,
    feats, wv, acc, xbuf, grad, term, outgo, income,
    w_sem, swap_sem, ring_send, ring_recv, part_sem, gp_sem, rs_send, rs_recv, out_sem,
):
    half = count // 2
    tok = x_ref.shape[1]
    piece = x_ref.shape[2]
    hidden = w_ref.shape[1]
    tiles = hidden // tile
    r = lax.axis_index("row")
    c = lax.axis_index("col")
    p = ring_place(c, count)
    near = (ring_column(p + 1, count), ring_column(p - 1, count))
    other = {"row": 1 - r}

    order = [0]
    for s in range(1, half + 1):
        order += [-s] if s == half else [-s, s]
    columns = {o: ring_column(p + o, count) for o in order}
    columns[half] = columns[-half]

    def rows_of(q):
        h = lax.rem(r + q, 2)
        return pl.ds(pl.multiple_of(h * tok, tok), tok)

    w_copies = {}
    for j, o in enumerate(order):
        k = columns[o]
        w_copies[o] = pltpu.make_async_copy(
            w_ref.at[pl.ds(pl.multiple_of(k * piece, piece), piece)], wv.at[k], w_sem.at[j]
        )
        w_copies[o].start()

    barrier = pltpu.get_barrier_semaphore()
    for target in ({"col": near[0]}, {"col": near[1]}, other):
        pl.semaphore_signal(barrier, inc=1, device_id=target, device_id_type=MESH)
    pl.semaphore_wait(barrier, 3)

    def ring_copy(d, s, q):
        o = -(s - 1) if d == 0 else s - 1
        k = columns[o]
        part = feats.at[k, rows_of(q)]
        return pltpu.make_async_remote_copy(
            src_ref=part, dst_ref=part,
            send_sem=ring_send.at[d, s - 1, q], recv_sem=ring_recv.at[d, s - 1, q],
            device_id={"col": near[d]}, device_id_type=MESH,
        )

    def ring_arrival(d, s, q):
        o = -s if d == 0 else s
        part = feats.at[columns[o], rows_of(q)]
        return pltpu.make_async_remote_copy(
            src_ref=part, dst_ref=part,
            send_sem=ring_send.at[d, s - 1, q], recv_sem=ring_recv.at[d, s - 1, q],
            device_id={"col": near[d]}, device_id_type=MESH,
        )

    def used(d, s, q):
        return s < half or (s == half and q == d)

    swap = pltpu.make_async_remote_copy(
        src_ref=x_ref.at[1 - r], dst_ref=feats.at[c, rows_of(0)],
        send_sem=swap_sem.at[0], recv_sem=swap_sem.at[1],
        device_id=other, device_id_type=MESH,
    )
    swap.start()
    feats[c, rows_of(0), :] = x_ref[r]
    sent = []
    for d in range(2):
        if used(d, 1, 0):
            copy = ring_copy(d, 1, 0)
            copy.start()
            sent.append(copy)
    arrived = pltpu.make_async_remote_copy(
        src_ref=x_ref.at[1 - r], dst_ref=feats.at[c, rows_of(1)],
        send_sem=swap_sem.at[0], recv_sem=swap_sem.at[1],
        device_id=other, device_id_type=MESH,
    )
    arrived.wait_recv()
    for d in range(2):
        if used(d, 1, 1):
            copy = ring_copy(d, 1, 1)
            copy.start()
            sent.append(copy)

    def project(o):
        k = columns[o]
        w_copies[o].wait()

        @pl.loop(0, tiles)
        def _(t):
            cols = pl.ds(pl.multiple_of(t * tile, tile), tile)
            product = jnp.dot(feats[k], wv[k, :, cols], preferred_element_type=jnp.float32)
            if o == 0:
                acc[t] = product
            else:
                acc[t] = acc[t] + product
            if o == order[-1]:
                part_copy(t).start()

    def part_copy(t):
        return pltpu.make_async_remote_copy(
            src_ref=acc.at[t, rows_of(1)], dst_ref=xbuf.at[t],
            send_sem=part_sem.at[0, t], recv_sem=part_sem.at[1, t],
            device_id=other, device_id_type=MESH,
        )

    pending = [0]
    for s in range(1, half + 1):
        for q in range(2):
            for d in range(2):
                if used(d, s, q):
                    ring_arrival(d, s, q).wait_recv()
                    if used(d, s + 1, q):
                        copy = ring_copy(d, s + 1, q)
                        copy.start()
                        sent.append(copy)
            if pending:
                project(pending.pop(0))
        for o in pending:
            project(o)
        pending = [-s] if s == half else [-s, s]
    for o in pending:
        project(o)

    own_copies = []
    for j, o in enumerate(order):
        k = columns[o]
        copy = pltpu.make_async_copy(
            feats.at[k], own_ref.at[:, pl.ds(pl.multiple_of(k * piece, piece), piece)], out_sem.at[j]
        )
        copy.start()
        own_copies.append(copy)

    mine, theirs = rows_of(0), rows_of(1)

    def grad_copy(t):
        part = grad.at[mine, pl.ds(pl.multiple_of(t * tile, tile), tile)]
        return pltpu.make_async_remote_copy(
            src_ref=part, dst_ref=part,
            send_sem=gp_sem.at[0, t], recv_sem=gp_sem.at[1, t],
            device_id=other, device_id_type=MESH,
        )

    @pl.loop(0, tiles)
    def _(t):
        cols = pl.ds(pl.multiple_of(t * tile, tile), tile)
        part_copy(t).wait_recv()
        value, slope = gelu_parts(acc[t, mine, :] + xbuf[t])
        act_ref[:, cols] = value.astype(act_ref.dtype)
        grad[mine, cols] = (ga_ref[:, cols].astype(jnp.float32) * slope).astype(grad.dtype)
        grad_copy(t).start()

    @pl.loop(0, tiles)
    def _(t):
        cols = pl.ds(pl.multiple_of(t * tile, tile), tile)
        part = grad.at[theirs, cols]
        pltpu.make_async_remote_copy(
            src_ref=part, dst_ref=part,
            send_sem=gp_sem.at[0, t], recv_sem=gp_sem.at[1, t],
            device_id=other, device_id_type=MESH,
        ).wait_recv()

    gradall_copy = pltpu.make_async_copy(grad, gradall_ref, out_sem.at[count])
    gradall_copy.start()

    def back_project(o, into):
        k = columns[o]

        @pl.loop(0, piece // split)
        def _(j):
            part = pl.ds(pl.multiple_of(j * split, split), split)
            into[:, part] = lax.dot_general(
                grad[...], wv[k, part, :], (((1,), (1,)), ((), ())),
                preferred_element_type=jnp.float32,
            )

    def sum_copy(d, s, q):
        return pltpu.make_async_remote_copy(
            src_ref=outgo.at[d, s - 1, rows_of(q)], dst_ref=income.at[d, s - 1, rows_of(q)],
            send_sem=rs_send.at[d, s - 1, q], recv_sem=rs_recv.at[d, s - 1, q],
            device_id={"col": near[d]}, device_id_type=MESH,
        )

    def sum_used(d, s, q):
        return s > 1 or q == d

    for s in range(1, half + 1):
        far = half - s + 1
        if s == 1:
            back_project(-far, term.at[0])
        else:
            back_project(far, term.at[0])
            back_project(-far, term.at[1])
        for late in (False, True):
            for q in range(2):
                for d in range(2):
                    if not sum_used(d, s, q):
                        continue
                    has_sum = s > 1 and sum_used(d, s - 1, q)
                    if has_sum != late:
                        continue
                    rows = rows_of(q)
                    value = term[0 if s == 1 else d, rows, :]
                    if has_sum:
                        sum_copy(d, s - 1, q).wait_recv()
                        value = value + income[d, s - 2, rows, :].astype(jnp.float32)
                    if s < half:
                        outgo[d, s - 1, rows, :] = value.astype(outgo.dtype)
                        copy = sum_copy(d, s, q)
                        copy.start()
                        sent.append(copy)
                    else:
                        sum_ref[d, rows, :] = value.astype(sum_ref.dtype)
    back_project(0, term_ref)

    swap.wait_send()
    for copy in sent:
        copy.wait_send()
    for copy in own_copies:
        copy.wait()
    gradall_copy.wait()

    @pl.loop(0, tiles)
    def _(t):
        part_copy(t).wait_send()
        grad_copy(t).wait_send()


def exchange(x_halves, weights, grad_act, count):
    _, tok, piece = x_halves.shape
    half_rows, hidden = weights.shape
    half = count // 2
    tile = 512 if hidden % 512 == 0 else 128
    split = 256 if piece % 256 == 0 else 128
    tiles = hidden // tile
    all_tok = 2 * tok
    vmem = pl.BlockSpec(memory_space=pltpu.VMEM)
    hbm = pl.BlockSpec(memory_space=pl.ANY)
    bf16, f32 = jnp.bfloat16, jnp.float32
    dma = pltpu.SemaphoreType.DMA
    return pl.pallas_call(
        functools.partial(exchange_kernel, count, tile, split),
        out_shape=(
            jax.ShapeDtypeStruct((tok, hidden), bf16),
            jax.ShapeDtypeStruct((all_tok, half_rows), bf16),
            jax.ShapeDtypeStruct((all_tok, hidden), bf16),
            jax.ShapeDtypeStruct((2, all_tok, piece), bf16),
            jax.ShapeDtypeStruct((all_tok, piece), f32),
        ),
        in_specs=[vmem, hbm, vmem],
        out_specs=(vmem, hbm, hbm, vmem, vmem),
        scratch_shapes=[
            pltpu.VMEM((count, all_tok, piece), bf16),
            pltpu.VMEM((count, piece, hidden), bf16),
            pltpu.VMEM((tiles, all_tok, tile), f32),
            pltpu.VMEM((tiles, tok, tile), f32),
            pltpu.VMEM((all_tok, hidden), bf16),
            pltpu.VMEM((2, all_tok, piece), f32),
            pltpu.VMEM((2, half - 1, all_tok, piece), bf16),
            pltpu.VMEM((2, half - 1, all_tok, piece), bf16),
            dma((count,)),
            dma((2,)),
            dma((2, half, 2)),
            dma((2, half, 2)),
            dma((2, tiles)),
            dma((2, tiles)),
            dma((2, half - 1, 2)),
            dma((2, half - 1, 2)),
            dma((count + 1,)),
        ],
        compiler_params=pltpu.CompilerParams(
            collective_id=0, has_side_effects=True, vmem_limit_bytes=62 * 1024 * 1024
        ),
        cost_estimate=pl.CostEstimate(
            flops=4 * all_tok * half_rows * hidden,
            bytes_accessed=2 * half_rows * hidden,
            transcendentals=tok * hidden,
        ),
    )(x_halves, weights, grad_act)


def weight_gradient(own_half, grad_all):
    return lax.dot_general(
        own_half, grad_all, (((0,), (0,)), ((), ())), preferred_element_type=jnp.float32
    ).astype(jnp.bfloat16)


def local(inputs, weights, grad_act):
    tok_rows, row_count, piece_cols = inputs.shape
    all_tokens = tok_rows * row_count
    col_count = lax.axis_size("col")
    x_halves = jnp.transpose(inputs, (1, 0, 2))
    activation, own_half, grad_all, sums, own_term = exchange(x_halves, weights, grad_act, col_count)
    ring = [ring_column_static(place, col_count) for place in range(col_count)]
    onward = [(ring[i], ring[(i + 1) % col_count]) for i in range(col_count)]
    backward = [(target, source) for source, target in onward]
    from_left = lax.ppermute(sums[0], "col", onward)
    from_right = lax.ppermute(sums[1], "col", backward)
    grad_w = weight_gradient(own_half, grad_all)
    summed = own_term + from_left.astype(jnp.float32) + from_right.astype(jnp.float32)
    arranged = summed.astype(jnp.bfloat16).reshape(row_count, tok_rows, 1, piece_cols)
    moved = lax.all_to_all(arranged, "row", split_axis=0, concat_axis=2, tiled=True)
    return (activation, moved.reshape(tok_rows, row_count, piece_cols), grad_w)


def ring_column_static(place, count):
    return 2 * place if place < count // 2 else 2 * (count - 1 - place) + 1


def plain(inputs, weights, grad_act):
    tok_rows, row_count, piece_cols = inputs.shape
    half_rows, hid_cols = weights.shape
    all_tokens = tok_rows * row_count
    col_count = lax.axis_size("col")
    own = lax.all_to_all(inputs, "row", split_axis=1, concat_axis=0, tiled=True)
    own_half = lax.all_gather(own.reshape(all_tokens, piece_cols), "col", axis=1, tiled=True)
    partial = jnp.dot(own_half, weights, preferred_element_type=jnp.float32)
    preact = lax.psum_scatter(partial, "row", scatter_dimension=0, tiled=True)
    value, slope = gelu_parts(preact)
    activation = value.astype(jnp.bfloat16)
    grad_pre = (grad_act.astype(jnp.float32) * slope).astype(jnp.bfloat16)
    grad_all = lax.all_gather(grad_pre, "row", axis=0, tiled=True)
    grad_w = weight_gradient(own_half, grad_all)
    local_terms = lax.dot_general(
        grad_all, weights, (((1,), (1,)), ((), ())), preferred_element_type=jnp.float32
    )
    split_terms = local_terms.reshape(all_tokens, col_count, piece_cols)
    received = lax.all_to_all(split_terms, "col", split_axis=1, concat_axis=1, tiled=True)
    summed = jnp.sum(received, axis=1).astype(jnp.bfloat16)
    arranged = summed.reshape(row_count, tok_rows, 1, piece_cols)
    moved = lax.all_to_all(arranged, "row", split_axis=0, concat_axis=2, tiled=True)
    return (activation, moved.reshape(tok_rows, row_count, piece_cols), grad_w)


def solution(mesh):
    placed = (P(("groups", "row"), None, "col"), P("row", "col"), P(("groups", "row"), "col"))

    def by_shape(inputs, weights, grad_act):
        tok_rows, row_count, piece_cols = inputs.shape
        hid_cols = weights.shape[1]
        fits = (
            row_count == 2
            and mesh.shape["col"] in (4, 6, 8)
            and tok_rows % 16 == 0
            and piece_cols % 128 == 0
            and hid_cols % 128 == 0
        )
        return (local if fits else plain)(inputs, weights, grad_act)

    return jax.shard_map(
        by_shape,
        mesh=mesh,
        in_specs=placed,
        out_specs=(
            P(("groups", "row"), "col"),
            P(("groups", "row"), None, "col"),
            P(("groups", "row"), "col"),
        ),
        check_vma=False,
    )
```

```python
import functools
import math

import jax
import jax.numpy as jnp
from jax import lax
from jax.experimental import pallas as pl
from jax.experimental.pallas import tpu as pltpu
from jax.sharding import PartitionSpec as P

root_coef = math.sqrt(2.0 / math.pi)
cube_coef = 0.044715
MESH = pl.DeviceIdType.MESH


def gelu_parts(preact):
    square = preact * preact
    tangent = jnp.tanh(root_coef * (preact + cube_coef * square * preact))
    half = 0.5 * (1.0 + tangent)
    slope = half + 0.5 * preact * (1.0 - tangent * tangent) * root_coef * (
        1.0 + 3.0 * cube_coef * square
    )
    return preact * half, slope


def ring_place(index, count):
    z, x = index // 2, index % 2
    return z * (1 - x) + (count - 1 - z) * x


def ring_column(place, count):
    place = lax.rem(place + 2 * count, count)
    back = place // (count // 2)
    return (1 - back) * (2 * place) + back * (2 * (count - 1 - place) + 1)


def exchange_kernel(
    count, tile, split,
    x_ref, w_ref, ga_ref,
    act_ref, own_ref, gradall_ref, sum_right, sum_left, term_right, term_left, term_mine, term_theirs,
    feats, wv, acc, xbuf, grad, term, outgo, income,
    w_sem, swap_sem, ring_send, ring_recv, part_sem, gp_sem, rs_send, rs_recv, out_sem,
):
    half = count // 2
    tok = x_ref.shape[1]
    piece = x_ref.shape[2]
    hidden = w_ref.shape[1]
    tiles = hidden // tile
    r = lax.axis_index("row")
    c = lax.axis_index("col")
    p = ring_place(c, count)
    near = (ring_column(p + 1, count), ring_column(p - 1, count))
    other = {"row": 1 - r}

    order = [0]
    for s in range(1, half + 1):
        order += [-s] if s == half else [-s, s]
    columns = {o: ring_column(p + o, count) for o in order}
    columns[half] = columns[-half]

    def rows_of(q):
        return pl.ds(q * tok, tok)

    w_copies = {}
    for j, o in enumerate(order):
        k = columns[o]
        w_copies[o] = pltpu.make_async_copy(
            w_ref.at[pl.ds(pl.multiple_of(k * piece, piece), piece)], wv.at[k], w_sem.at[j]
        )
        w_copies[o].start()

    barrier = pltpu.get_barrier_semaphore()
    for target in ({"col": near[0]}, {"col": near[1]}, other):
        pl.semaphore_signal(barrier, inc=1, device_id=target, device_id_type=MESH)
    pl.semaphore_wait(barrier, 3)

    def ring_copy(d, s, q):
        o = -(s - 1) if d == 0 else s - 1
        k = columns[o]
        part = feats.at[k, rows_of(q)]
        return pltpu.make_async_remote_copy(
            src_ref=part, dst_ref=part,
            send_sem=ring_send.at[d, s - 1, q], recv_sem=ring_recv.at[d, s - 1, q],
            device_id={"col": near[d]}, device_id_type=MESH,
        )

    def ring_arrival(d, s, q):
        o = -s if d == 0 else s
        part = feats.at[columns[o], rows_of(q)]
        return pltpu.make_async_remote_copy(
            src_ref=part, dst_ref=part,
            send_sem=ring_send.at[d, s - 1, q], recv_sem=ring_recv.at[d, s - 1, q],
            device_id={"col": near[d]}, device_id_type=MESH,
        )

    def used(d, s, q):
        return s < half or (s == half and q == d)

    swap = pltpu.make_async_remote_copy(
        src_ref=x_ref.at[1 - r], dst_ref=feats.at[c, rows_of(1)],
        send_sem=swap_sem.at[0], recv_sem=swap_sem.at[1],
        device_id=other, device_id_type=MESH,
    )
    swap.start()
    feats[c, rows_of(0), :] = x_ref[r]
    sent = []
    for d in range(2):
        if used(d, 1, 0):
            copy = ring_copy(d, 1, 0)
            copy.start()
            sent.append(copy)
    swap.wait_recv()
    for d in range(2):
        if used(d, 1, 1):
            copy = ring_copy(d, 1, 1)
            copy.start()
            sent.append(copy)

    def project(o):
        k = columns[o]
        w_copies[o].wait()

        @pl.loop(0, tiles)
        def _(t):
            cols = pl.ds(pl.multiple_of(t * tile, tile), tile)
            product = jnp.dot(feats[k], wv[k, :, cols], preferred_element_type=jnp.float32)
            if o == 0:
                acc[t] = product
            else:
                acc[t] = acc[t] + product
            if o == order[-1]:
                part_copy(t).start()

    def part_copy(t):
        return pltpu.make_async_remote_copy(
            src_ref=acc.at[t, rows_of(1)], dst_ref=xbuf.at[t],
            send_sem=part_sem.at[0, t], recv_sem=part_sem.at[1, t],
            device_id=other, device_id_type=MESH,
        )

    pending = [0]
    for s in range(1, half + 1):
        for q in range(2):
            for d in range(2):
                if used(d, s, q):
                    ring_arrival(d, s, q).wait_recv()
                    if used(d, s + 1, q):
                        copy = ring_copy(d, s + 1, q)
                        copy.start()
                        sent.append(copy)
            if pending:
                project(pending.pop(0))
        for o in pending:
            project(o)
        pending = [-s] if s == half else [-s, s]
    for o in pending:
        project(o)

    own_copies = []
    for j, o in enumerate(order):
        k = columns[o]
        copy = pltpu.make_async_copy(
            feats.at[k], own_ref.at[:, pl.ds(pl.multiple_of(k * piece, piece), piece)], out_sem.at[j]
        )
        copy.start()
        own_copies.append(copy)

    mine, theirs = rows_of(0), rows_of(1)

    def grad_copy(t):
        cols = pl.ds(pl.multiple_of(t * tile, tile), tile)
        return pltpu.make_async_remote_copy(
            src_ref=grad.at[mine, cols], dst_ref=grad.at[theirs, cols],
            send_sem=gp_sem.at[0, t], recv_sem=gp_sem.at[1, t],
            device_id=other, device_id_type=MESH,
        )

    @pl.loop(0, tiles)
    def _(t):
        cols = pl.ds(pl.multiple_of(t * tile, tile), tile)
        part_copy(t).wait_recv()
        value, slope = gelu_parts(acc[t, mine, :] + xbuf[t])
        act_ref[:, cols] = value.astype(act_ref.dtype)
        grad[mine, cols] = (ga_ref[:, cols].astype(jnp.float32) * slope).astype(grad.dtype)
        grad_copy(t).start()

    @pl.loop(0, tiles)
    def _(t):
        grad_copy(t).wait_recv()

    gradall_copy = pltpu.make_async_copy(grad, gradall_ref, out_sem.at[count])
    gradall_copy.start()

    def back_project(o, into):
        k = columns[o]

        @pl.loop(0, piece // split)
        def _(j):
            part = pl.ds(pl.multiple_of(j * split, split), split)
            value = lax.dot_general(
                wv[k, part, :], grad[...], (((1,), (1,)), ((), ())),
                preferred_element_type=jnp.float32,
            )
            if len(into) == 1:
                into[0][part, :] = value
            else:
                into[0][part, :] = value[:, :tok]
                into[1][part, :] = value[:, tok:]

    def feature_rows(q):
        return pl.ds(q * (piece // 2), piece // 2)

    def sum_copy(d, s, q):
        return pltpu.make_async_remote_copy(
            src_ref=outgo.at[d, s - 1, feature_rows(q)], dst_ref=income.at[d, s - 1, feature_rows(q)],
            send_sem=rs_send.at[d, s - 1, q], recv_sem=rs_recv.at[d, s - 1, q],
            device_id={"col": near[d]}, device_id_type=MESH,
        )

    def sum_used(d, s, q):
        return s > 1 or q == d

    for s in range(1, half):
        far = half - s + 1
        if s == 1:
            back_project(-far, [term.at[0]])
        else:
            back_project(far, [term.at[0]])
            back_project(-far, [term.at[1]])
        if s == half - 1:
            back_project(1, [term_right])
            back_project(-1, [term_left])
        for late in (False, True):
            for q in range(2):
                for d in range(2):
                    if not sum_used(d, s, q):
                        continue
                    has_sum = s > 1 and sum_used(d, s - 1, q)
                    if has_sum != late:
                        continue
                    rows = feature_rows(q)
                    value = term[0 if s == 1 else d, rows, :]
                    if has_sum:
                        sum_copy(d, s - 1, q).wait_recv()
                        value = value + income[d, s - 2, rows, :].astype(jnp.float32)
                    if s < half - 1:
                        outgo[d, s - 1, rows, :] = value.astype(outgo.dtype)
                        copy = sum_copy(d, s, q)
                        copy.start()
                        sent.append(copy)
                    else:
                        (sum_right, sum_left)[d][rows, :] = value.astype(sum_right.dtype)
        if s == half - 2:
            back_project(0, [term_mine, term_theirs])

    swap.wait_send()
    for copy in sent:
        copy.wait_send()
    for copy in own_copies:
        copy.wait()
    gradall_copy.wait()

    @pl.loop(0, tiles)
    def _(t):
        part_copy(t).wait_send()
        grad_copy(t).wait_send()


def exchange(x_halves, weights, grad_act, count):
    _, tok, piece = x_halves.shape
    half_rows, hidden = weights.shape
    half = count // 2
    tile = 512 if hidden % 512 == 0 else 128
    split = piece
    tiles = hidden // tile
    all_tok = 2 * tok
    vmem = pl.BlockSpec(memory_space=pltpu.VMEM)
    hbm = pl.BlockSpec(memory_space=pl.ANY)
    bf16, f32 = jnp.bfloat16, jnp.float32
    dma = pltpu.SemaphoreType.DMA
    return pl.pallas_call(
        functools.partial(exchange_kernel, count, tile, split),
        out_shape=(
            jax.ShapeDtypeStruct((tok, hidden), bf16),
            jax.ShapeDtypeStruct((all_tok, half_rows), bf16),
            jax.ShapeDtypeStruct((all_tok, hidden), bf16),
            jax.ShapeDtypeStruct((piece, all_tok), bf16),
            jax.ShapeDtypeStruct((piece, all_tok), bf16),
            jax.ShapeDtypeStruct((piece, all_tok), f32),
            jax.ShapeDtypeStruct((piece, all_tok), f32),
            jax.ShapeDtypeStruct((piece, tok), f32),
            jax.ShapeDtypeStruct((piece, tok), f32),
        ),
        in_specs=[vmem, hbm, vmem],
        out_specs=(vmem, hbm, hbm) + (vmem,) * 6,
        scratch_shapes=[
            pltpu.VMEM((count, all_tok, piece), bf16),
            pltpu.VMEM((count, piece, hidden), bf16),
            pltpu.VMEM((tiles, all_tok, tile), f32),
            pltpu.VMEM((tiles, tok, tile), f32),
            pltpu.VMEM((all_tok, hidden), bf16),
            pltpu.VMEM((2, piece, all_tok), f32),
            pltpu.VMEM((2, half - 2, piece, all_tok), bf16),
            pltpu.VMEM((2, half - 2, piece, all_tok), bf16),
            dma((count,)),
            dma((2,)),
            dma((2, half, 2)),
            dma((2, half, 2)),
            dma((2, tiles)),
            dma((2, tiles)),
            dma((2, half - 2, 2)),
            dma((2, half - 2, 2)),
            dma((count + 1,)),
        ],
        compiler_params=pltpu.CompilerParams(
            collective_id=0, has_side_effects=True, vmem_limit_bytes=62 * 1024 * 1024
        ),
        cost_estimate=pl.CostEstimate(
            flops=4 * all_tok * half_rows * hidden,
            bytes_accessed=2 * half_rows * hidden,
            transcendentals=tok * hidden,
        ),
    )(x_halves, weights, grad_act)


def weight_gradient(own_half, grad_all):
    return lax.dot_general(
        own_half, grad_all, (((0,), (0,)), ((), ())), preferred_element_type=jnp.float32
    ).astype(jnp.bfloat16)


def gradient_kernel(own_ref, grad_ref, *rest):
    out_ref = rest[-1]
    out_ref[...] = lax.dot_general(
        own_ref[...], grad_ref[...], (((0,), (0,)), ((), ())), preferred_element_type=jnp.float32
    ).astype(out_ref.dtype)


def gradient_rows(own_half, grad_all, block, first, blocks, filled=None):
    tokens, features = own_half.shape
    hidden = grad_all.shape[1]
    in_specs = [
        pl.BlockSpec((tokens, block), lambda i: (0, i + first)),
        pl.BlockSpec((tokens, hidden), lambda i: (0, 0)),
    ]
    operands = [own_half, grad_all]
    if filled is not None:
        in_specs.append(pl.BlockSpec(memory_space=pl.ANY))
        operands.append(filled)
    return pl.pallas_call(
        gradient_kernel,
        grid=(blocks,),
        out_shape=jax.ShapeDtypeStruct((features, hidden), jnp.bfloat16),
        in_specs=in_specs,
        out_specs=pl.BlockSpec((block, hidden), lambda i: (i + first, 0)),
        input_output_aliases={} if filled is None else {2: 0},
        compiler_params=pltpu.CompilerParams(vmem_limit_bytes=60 * 1024 * 1024),
        cost_estimate=pl.CostEstimate(
            flops=2 * tokens * block * blocks * hidden,
            bytes_accessed=2 * (block * blocks * (hidden + tokens) + tokens * hidden),
            transcendentals=0,
        ),
    )(*operands)


def local(inputs, weights, grad_act):
    tok, _, piece = inputs.shape
    half_rows = weights.shape[0]
    count = lax.axis_size("col")
    f32, bf16 = jnp.float32, jnp.bfloat16
    x_halves = jnp.transpose(inputs, (1, 0, 2))
    (
        activation, own_half, grad_all,
        sum_right, sum_left, term_right, term_left, term_mine, term_theirs,
    ) = exchange(x_halves, weights, grad_act, count)
    ring = [ring_column_static(place, count) for place in range(count)]
    onward = [(ring[i], ring[(i + 1) % count]) for i in range(count)]
    backward = [(target, source) for source, target in onward]
    crossed = [
        [(row * count + a, (1 - row) * count + b) for row in range(2) for a, b in hops]
        for hops in (onward, backward)
    ]
    from_left = lax.ppermute(sum_right, "col", onward)
    from_right = lax.ppermute(sum_left, "col", backward)
    theirs_own = lax.ppermute(term_theirs, "row", [(0, 1), (1, 0)])
    first = count // 2
    grad_w = gradient_rows(own_half, grad_all, piece, 0, first)
    to_right = (term_right + from_left.astype(f32)).astype(bf16)
    to_left = (term_left + from_right.astype(f32)).astype(bf16)
    mine = [
        lax.ppermute(to_right[:, :tok], "col", onward),
        lax.ppermute(to_left[:, :tok], "col", backward),
    ]
    theirs = [
        lax.ppermute(to_right[:, tok:], ("row", "col"), crossed[0]),
        lax.ppermute(to_left[:, tok:], ("row", "col"), crossed[1]),
    ]
    grad_w = gradient_rows(own_half, grad_all, piece, first, count - first, grad_w)
    mine = (term_mine + mine[0].astype(f32) + mine[1].astype(f32)).astype(bf16)
    theirs = (theirs_own + theirs[0].astype(f32) + theirs[1].astype(f32)).astype(bf16)
    upper = lax.axis_index("row") == 0
    halves = jnp.stack([jnp.where(upper, mine, theirs), jnp.where(upper, theirs, mine)])
    grad_x = jnp.transpose(halves, (2, 0, 1))
    return (activation, grad_x, grad_w)


def ring_column_static(place, count):
    return 2 * place if place < count // 2 else 2 * (count - 1 - place) + 1


def plain(inputs, weights, grad_act):
    tok_rows, row_count, piece_cols = inputs.shape
    half_rows, hid_cols = weights.shape
    all_tokens = tok_rows * row_count
    col_count = lax.axis_size("col")
    own = lax.all_to_all(inputs, "row", split_axis=1, concat_axis=0, tiled=True)
    own_half = lax.all_gather(own.reshape(all_tokens, piece_cols), "col", axis=1, tiled=True)
    partial = jnp.dot(own_half, weights, preferred_element_type=jnp.float32)
    preact = lax.psum_scatter(partial, "row", scatter_dimension=0, tiled=True)
    value, slope = gelu_parts(preact)
    activation = value.astype(jnp.bfloat16)
    grad_pre = (grad_act.astype(jnp.float32) * slope).astype(jnp.bfloat16)
    grad_all = lax.all_gather(grad_pre, "row", axis=0, tiled=True)
    grad_w = weight_gradient(own_half, grad_all)
    local_terms = lax.dot_general(
        grad_all, weights, (((1,), (1,)), ((), ())), preferred_element_type=jnp.float32
    )
    split_terms = local_terms.reshape(all_tokens, col_count, piece_cols)
    received = lax.all_to_all(split_terms, "col", split_axis=1, concat_axis=1, tiled=True)
    summed = jnp.sum(received, axis=1).astype(jnp.bfloat16)
    arranged = summed.reshape(row_count, tok_rows, 1, piece_cols)
    moved = lax.all_to_all(arranged, "row", split_axis=0, concat_axis=2, tiled=True)
    return (activation, moved.reshape(tok_rows, row_count, piece_cols), grad_w)


def solution(mesh):
    placed = (P(("groups", "row"), None, "col"), P("row", "col"), P(("groups", "row"), "col"))

    def by_shape(inputs, weights, grad_act):
        tok_rows, row_count, piece_cols = inputs.shape
        hid_cols = weights.shape[1]
        fits = (
            row_count == 2
            and mesh.shape["col"] in (6, 8, 10)
            and tok_rows % 16 == 0
            and piece_cols % 128 == 0
            and hid_cols % 128 == 0
        )
        return (local if fits else plain)(inputs, weights, grad_act)

    return jax.shard_map(
        by_shape,
        mesh=mesh,
        in_specs=placed,
        out_specs=(
            P(("groups", "row"), "col"),
            P(("groups", "row"), None, "col"),
            P(("groups", "row"), "col"),
        ),
        check_vma=False,
    )
```
